256 devices in a mesh: pipe: 16 (over x_hi, y, core), ctx: 16 (over x_lo, z).
Axes of the slice: x: 4 (x_hi: 2, x_lo: 2; x = x_hi * 2 + x_lo), y: 4, z: 8, core: 2. Of those that a mesh axis runs over, the one named last changes fastest.
Arguments:
- query: bfloat16 [16, 2048, 4096], P('pipe', 'ctx'), may hold values from -8 to 8
- key: bfloat16 [16, 2048, 512], P('pipe', 'ctx'), may hold values from -8 to 8
- value: bfloat16 [16, 2048, 512], P('pipe', 'ctx'), may hold values from -6 to 6
- out_grad: bfloat16 [16, 2048, 4096], P('pipe', 'ctx'), may hold values from -6 to 6
- positions: int32 [16, 2048], P('pipe', 'ctx'), may hold values from 0 to 2047, as said below
- gains: float32 [16, 2, 128], P('pipe'), may hold values from 0.5 to 5, as said below
Outputs:
- attended: bfloat16 [16, 2048, 4096], P('pipe', 'ctx')
- query_grad: bfloat16 [16, 2048, 4096], P('pipe', 'ctx')
- key_grad: bfloat16 [16, 2048, 512], P('pipe', 'ctx')
- value_grad: bfloat16 [16, 2048, 512], P('pipe', 'ctx')
- gain_grad: float32 [16, 2, 128], P('pipe')
The draws below stay inside these ranges and needn't reach their ends.
Inputs may be any that keep to these rules, and one draw needn't show every extreme that they name: Row p holds the positions of sequence p, each position once; the 128 rows of one device are two runs of 64 consecutive, increasing positions that start at multiples of 64; the 32 runs may lie on the devices in any order. `gains`: rows p and 15 - p are equal.
All inputs are finite; a program needn't handle non-finite values.
Results may differ from the reference program's by a relative error of at most 0.03.
The reference program's roundings to bfloat16 on the way (of `q_rot`, `k_rot` and `d_score`) count: a program that leaves them out, or rounds other values in their place, can miss the bound.
Values may be sent and summed in bfloat16 or wider, within the bound.
No kernel may reach another device: no remote copies, remote signals or barrier semaphores. Data moves between devices by JAX's collectives and lax.ppermute only.
A program may use at most 192 MiB of HBM per device.

```python
import jax
import jax.numpy as jnp
from jax import lax

HQ = 32
HK = 4
DH = 128
TOK_DEV = 128
SEQ = 2048
RUNS = 32
PIPES = 16


def key_field(key, stretch):
    base = jax.random.normal(key, (PIPES, SEQ, HK * DH), jnp.float32)
    spread = jnp.exp(jax.random.uniform(jax.random.fold_in(key, 7), (PIPES, SEQ, 1), jnp.float32, 0.0, stretch))
    return jnp.clip(base * spread, -8.0, 8.0)


def draw_key(key, part):
    field = key_field(key, 0.0)
    return field.astype(jnp.bfloat16)


def draw_query(key, part):
    key = jax.random.fold_in(key, 2)
    fresh = jax.random.normal(key, (PIPES, SEQ, HQ * DH), jnp.float32)
    return jnp.clip(fresh, -8.0, 8.0).astype(jnp.bfloat16)


def run_order(single):
    return jax.random.permutation(single, RUNS)


def draw_positions(key, part):
    key = jax.random.fold_in(key, 5)
    keys = jax.random.split(key, PIPES)
    order = jax.vmap(run_order)(keys).astype(jnp.int32)
    runs = order[:, :, None] * (TOK_DEV // 2) + jnp.arange(TOK_DEV // 2, dtype=jnp.int32)[None, None, :]
    return runs.reshape(PIPES, SEQ).astype(jnp.int32)


def draw_gains(key, part):
    key = jax.random.fold_in(key, 6)
    half = jnp.exp(jax.random.uniform(key, (PIPES // 2, 2, DH), jnp.float32, -0.69, 0.69))
    return jnp.concatenate([half, half[::-1]], 0)


def block_levels(own_key, shape, shards, smallest, top_value):
    def one(position, blocks):
        steps = jax.random.uniform(jax.random.fold_in(jax.random.fold_in(own_key, 6), position), (blocks,), jnp.float32, smallest / len(shards), top_value / len(shards))
        return jnp.repeat(jnp.exp(steps), shape[position] // blocks).reshape((-1,) + (1,) * (len(shape) - position - 1))

    level = one(*shards[0])
    for cut in shards[1:]:
        level = level * one(*cut)
    return level


def noise(rng, shape, scale, limit, cuts=(), held_as=jnp.bfloat16):
    result = scale * jax.random.normal(rng, shape, jnp.float32)
    if cuts:
        result = result * block_levels(rng, shape, cuts, -0.22, 0.18)
    return jnp.clip(result, -limit, limit).astype(held_as)


def setup_inputs(seed: int = 0) -> dict:
    key_of = jax.random.split(jax.random.key(seed), 7)
    return {
        "query": draw_query(jax.random.fold_in(key_of[6], 71), 0),
        "key": draw_key(jax.random.fold_in(key_of[6], 71), 0),
        "value": noise(key_of[2], (PIPES, SEQ, HK * DH), 1.0, 6.0, ((0, 16), (1, 16))),
        "out_grad": noise(key_of[3], (PIPES, SEQ, HQ * DH), 1.0, 6.0, ((0, 16), (1, 16))),
        "positions": draw_positions(jax.random.fold_in(key_of[6], 71), 0),
        "gains": draw_gains(jax.random.fold_in(key_of[6], 71), 0),
    }


THETA = 1000000.0
EPS = 1e-06
NEG = -1e+30

def rounded(x):
    return lax.optimization_barrier(x.astype(jnp.bfloat16)).astype(jnp.float32)

def angles(pos):
    freq = THETA ** (-(jnp.arange(DH // 2, dtype=jnp.float32) * 2.0) / DH)
    turn = pos.astype(jnp.float32)[:, None] * freq[None, :]
    return (jnp.cos(turn)[:, None, :], jnp.sin(turn)[:, None, :])

def rotate(x, cosine, sine):
    first, second = (x[..., :DH // 2], x[..., DH // 2:])
    return jnp.concatenate([first * cosine - second * sine, second * cosine + first * sine], -1)

def unrotate(x, cosine, sine):
    first, second = (x[..., :DH // 2], x[..., DH // 2:])
    return jnp.concatenate([first * cosine + second * sine, second * cosine - first * sine], -1)

def normalize(x, gain):
    inverse = lax.rsqrt(lax.optimization_barrier(jnp.mean(x * x, -1, keepdims=True)) + EPS)
    normed = x * inverse
    return (normed, inverse, normed * gain)

def norm_back(grad_scaled, normed, inverse, gain):
    grad_normed = grad_scaled * gain
    inner = lax.optimization_barrier(jnp.mean(grad_normed * normed, -1, keepdims=True))
    return inverse * (grad_normed - normed * inner)

def one_sequence(items):
    query, key, value, out_grad, pos, gains = items
    ratio = HQ // HK
    scale = DH ** (-0.5)
    cosine, sine = angles(pos)
    q_normed, q_inverse, q_scaled = normalize(query.astype(jnp.float32).reshape(SEQ, HQ, DH), gains[0])
    k_normed, k_inverse, k_scaled = normalize(key.astype(jnp.float32).reshape(SEQ, HK, DH), gains[1])
    q_rot = rotate(q_scaled, cosine, sine).astype(jnp.bfloat16).reshape(SEQ, HK, ratio, DH)
    k_rot = rotate(k_scaled, cosine, sine).astype(jnp.bfloat16)
    values = value.reshape(SEQ, HK, DH)
    grads = out_grad.reshape(SEQ, HK, ratio, DH)
    allowed = pos[None, :] <= pos[:, None]

    def group(parts):
        q_head, k_head, v_head, g_head = parts
        q_f = q_head.astype(jnp.float32)
        k_f = k_head.astype(jnp.float32)
        v_f = v_head.astype(jnp.float32)
        g_f = g_head.astype(jnp.float32)
        scores = jnp.einsum('qrd,kd->qrk', q_f, k_f) * scale
        scores = jnp.where(allowed[:, None, :], scores, NEG)
        top = lax.optimization_barrier(jnp.max(scores, -1, keepdims=True))
        expo = jnp.exp(scores - top)
        total = lax.optimization_barrier(jnp.sum(expo, -1, keepdims=True))
        attended = (jnp.einsum('qrk,kd->qrd', rounded(expo), v_f) / total).astype(jnp.bfloat16)
        logsum = top + jnp.log(total)
        probs = jnp.exp(scores - logsum)
        delta = lax.optimization_barrier(jnp.sum(g_f * lax.optimization_barrier(attended).astype(jnp.float32), -1, keepdims=True))
        d_value = jnp.einsum('qrk,qrd->kd', rounded(probs), g_f)
        d_prob = jnp.einsum('qrd,kd->qrk', g_f, v_f)
        d_score = rounded(probs * (d_prob - delta))
        d_query = jnp.einsum('qrk,kd->qrd', d_score, k_f) * scale
        d_key = jnp.einsum('qrk,qrd->kd', d_score, q_f) * scale
        return (attended, d_query, d_key, d_value)
    attended, d_query, d_key, d_value = lax.map(group, (q_rot.transpose(1, 0, 2, 3), k_rot.transpose(1, 0, 2), values.transpose(1, 0, 2), grads.transpose(1, 0, 2, 3)))
    attended = attended.transpose(1, 0, 2, 3).reshape(SEQ, HQ * DH)
    dq_scaled = unrotate(d_query.transpose(1, 0, 2, 3).reshape(SEQ, HQ, DH), cosine, sine)
    dk_scaled = unrotate(d_key.transpose(1, 0, 2), cosine, sine)
    query_grad = norm_back(dq_scaled, q_normed, q_inverse, gains[0]).astype(jnp.bfloat16).reshape(SEQ, HQ * DH)
    key_grad = norm_back(dk_scaled, k_normed, k_inverse, gains[1]).astype(jnp.bfloat16).reshape(SEQ, HK * DH)
    value_grad = d_value.transpose(1, 0, 2).astype(jnp.bfloat16).reshape(SEQ, HK * DH)
    own = jnp.stack([lax.optimization_barrier(jnp.sum(dq_scaled * q_normed, axis=(0, 1))), lax.optimization_barrier(jnp.sum(dk_scaled * k_normed, axis=(0, 1)))])
    return (attended, query_grad, key_grad, value_grad, own)

def reference(query, key, value, out_grad, positions, gains):
    attended, query_grad, key_grad, value_grad, own = lax.map(one_sequence, (query, key, value, out_grad, positions, gains))
    gain_grad = own + own[::-1]
    return (attended, query_grad, key_grad, value_grad, gain_grad)
```

```python
import functools

import jax
import jax.numpy as jnp
import numpy as np
from jax import lax
from jax.experimental import pallas as pl
from jax.experimental.pallas import tpu as pltpu
from jax.sharding import PartitionSpec as P

HQ = 32
HK = 4
DH = 128
THETA = 1000000.0
EPS = 1e-06
NEG = -1e30

TOK = 128
RUN = 64
SEQ = 2048
PAD = 16
GROUP = 8
QROWS = RUN * GROUP
KB = 256
NKB = SEQ // KB
HALF = HQ * DH // 2
SCALE = DH**-0.5
SCALE2 = SCALE * 1.4426950408889634
SHARDS = 16


def rope_table():
    freq = (THETA ** (-(np.arange(DH // 2, dtype=np.float64) * 2.0) / DH)).astype(np.float32)
    turn = np.arange(SEQ, dtype=np.float32)[:, None] * freq[None, :]
    turn = turn.astype(np.float64)
    return np.concatenate([np.cos(turn), np.sin(turn)], -1).astype(np.float32)


def dot(a, b, dims=((1,), (0,))):
    return lax.dot_general(a, b, (dims, ((), ())), preferred_element_type=jnp.float32)


NT = ((1,), (1,))


def cos_sin(tab):
    low = lax.broadcasted_iota(jnp.int32, tab.shape, 1) < DH // 2
    other = pltpu.roll(tab, DH // 2, 1)
    return jnp.where(low, tab, other), jnp.where(low, -other, tab)


def turn_by(x, cosine, sine):
    return x * cosine + pltpu.roll(x, DH // 2, 1) * sine


def turn_back(x, cosine, sine):
    return x * cosine - pltpu.roll(x, DH // 2, 1) * sine


def prep_kernel(pos, side, key, value, tab, gains, mine, other):
    run = pl.program_id(0)
    cosine, sine = cos_sin(tab[...])
    gain = gains[0, 1:2, :]
    pieces = []
    for head in range(HK):
        x = key[0, :, head * DH : (head + 1) * DH].astype(jnp.float32)
        inverse = lax.rsqrt(jnp.mean(x * x, -1, keepdims=True) + EPS)
        pieces.append(turn_by(x * inverse * gain, cosine, sine).astype(jnp.bfloat16))
    v = value[0]
    first = jnp.concatenate(pieces[:2] + [v[:, : 2 * DH]], -1)
    second = jnp.concatenate(pieces[2:] + [v[:, 2 * DH :]], -1)
    upper = side[0] == 1
    rows = pl.ds(pl.multiple_of(run * RUN, RUN), RUN)
    mine[rows, :] = jnp.where(upper, second, first)
    other[rows, :] = jnp.where(upper, first, second)

    @pl.when(run == 0)
    def _():
        lane = lax.broadcasted_iota(jnp.int32, (PAD, 4 * DH), 1)
        a = (pos[0, 0] // RUN).astype(jnp.float32)
        b = (pos[0, RUN] // RUN).astype(jnp.float32)
        tail = jnp.where(lane == 0, a, jnp.where(lane == 1, b, 0.0)).astype(jnp.bfloat16)
        mine[TOK:, :] = tail
        other[TOK:, :] = tail


def prep(positions, side, key, value, tab, gains):
    block = jax.ShapeDtypeStruct((TOK + PAD, 4 * DH), jnp.bfloat16)
    whole = pl.BlockSpec((TOK + PAD, 4 * DH), lambda r, p, s: (0, 0))
    return pl.pallas_call(
        prep_kernel,
        out_shape=(block, block),
        grid_spec=pltpu.PrefetchScalarGridSpec(
            num_scalar_prefetch=2,
            grid=(2,),
            in_specs=[
                pl.BlockSpec((1, RUN, HK * DH), lambda r, p, s: (0, r, 0)),
                pl.BlockSpec((1, RUN, HK * DH), lambda r, p, s: (0, r, 0)),
                pl.BlockSpec((RUN, DH), lambda r, p, s: (p[0, r * RUN] // RUN, 0)),
                pl.BlockSpec((1, 2, DH), lambda r, p, s: (0, 0, 0)),
            ],
            out_specs=(whole, whole),
        ),
        name="prep",
    )(positions, side, key, value, tab, gains)


def attention_kernel(blk, side, *refs):
    q_own, q_far, g_own, g_far, tab, gains = refs[:6]
    shards = refs[6 : 6 + SHARDS]
    att_own, att_far, dq_own, dq_far = refs[6 + SHARDS : 10 + SHARDS]
    outs = refs[10 + SHARDS : 10 + 2 * SHARDS]
    (own_out, ks, vs, kt, vt, scores, probs, dk, dv, o_acc, dq_acc, own_q, own_k) = refs[10 + 2 * SHARDS :]
    head = pl.program_id(0)
    run = pl.program_id(1)

    @pl.when(run == 0)
    def _():
        for a in range(SHARDS):
            k_all = jnp.where(head == 0, shards[a][:TOK, :DH], shards[a][:TOK, DH : 2 * DH])
            v_all = jnp.where(head == 0, shards[a][:TOK, 2 * DH : 3 * DH], shards[a][:TOK, 3 * DH :])
            for b in range(2):
                to = pl.ds(pl.multiple_of(blk[2 * a + b] * RUN, RUN), RUN)
                ks[to, :] = k_all[b * RUN : (b + 1) * RUN]
                vs[to, :] = v_all[b * RUN : (b + 1) * RUN]
        for j in range(NKB):
            kt[j] = ks[j * KB : (j + 1) * KB, :].T
            vt[j] = vs[j * KB : (j + 1) * KB, :].T
        dk[...] = jnp.zeros_like(dk)
        dv[...] = jnp.zeros_like(dv)

    @pl.when((run == 0) & (head == 0))
    def _():
        own_q[...] = jnp.zeros_like(own_q)
        own_k[...] = jnp.zeros_like(own_k)

    own = run < 2

    def stacked(near, far):
        x = jnp.where(own, near[0], far[...])
        return jnp.concatenate([x[:, h * DH : (h + 1) * DH] for h in range(GROUP)], 0)

    number = blk[run]
    cosine, sine = cos_sin(tab[pl.ds(pl.multiple_of(number * RUN, RUN), RUN), :])
    cosine = jnp.concatenate([cosine] * GROUP, 0)
    sine = jnp.concatenate([sine] * GROUP, 0)
    gain = gains[0, 0:1, :]
    x = stacked(q_own, q_far).astype(jnp.float32)
    q_inverse = lax.rsqrt(jnp.mean(x * x, -1, keepdims=True) + EPS)
    q_normed = x * q_inverse
    q_rot = turn_by(q_normed * gain, cosine, sine).astype(jnp.bfloat16)
    q_t = q_rot.T
    g_t = stacked(g_own, g_far).T

    last = number // (KB // RUN)
    lane = lax.broadcasted_iota(jnp.int32, (KB, QROWS), 1)
    row = lax.broadcasted_iota(jnp.int32, (KB, QROWS), 0)
    seen = row + last * KB <= number * RUN + (lane & (RUN - 1))

    def at(j):
        return pl.ds(pl.multiple_of(j * KB, KB), KB)

    def score(j):
        return dot(ks[at(j), :], q_t) * SCALE2

    def fold(x, op):
        return op(x.reshape(KB // 8, 8, QROWS), 0)

    s = jnp.where(seen, score(last), NEG)
    scores[at(last), :] = s

    def pass_a(j, top):
        s = score(j)
        scores[at(j), :] = s
        return jnp.maximum(top, fold(s, jnp.max))

    top = lax.fori_loop(0, last, pass_a, fold(s, jnp.max))
    top = jnp.max(top, 0, keepdims=True)

    o_acc[...] = jnp.zeros_like(o_acc)

    def pass_b(j, total):
        expo = jnp.exp2(scores[at(j), :] - top)
        low = expo.astype(jnp.bfloat16)
        probs[at(j), :] = low
        o_acc[...] += dot(vt[j], low)
        return total + fold(expo, jnp.sum)

    total = lax.fori_loop(0, last + 1, pass_b, jnp.zeros((8, QROWS), jnp.float32))
    inverse = 1.0 / jnp.sum(total, 0, keepdims=True)
    att_t = (o_acc[...] * inverse).astype(jnp.bfloat16)
    g_low = (g_t.astype(jnp.float32) * inverse).astype(jnp.bfloat16)
    delta = jnp.sum(g_low.astype(jnp.float32) * att_t.astype(jnp.float32), 0, keepdims=True)

    def unstacked(x):
        return jnp.concatenate([x[h * RUN : (h + 1) * RUN] for h in range(GROUP)], 1)

    att = unstacked(att_t.T)

    dq_acc[...] = jnp.zeros_like(dq_acc)

    def pass_c(j, carry):
        p = probs[at(j), :]
        d_prob = dot(vs[at(j), :], g_low)
        d_score = (p.astype(jnp.float32) * (d_prob - delta)).astype(jnp.bfloat16)
        dv[at(j), :] += dot(p, g_low, NT)
        dk[at(j), :] += dot(d_score, q_t, NT)
        dq_acc[...] += dot(kt[j], d_score)
        return carry

    lax.fori_loop(0, last + 1, pass_c, 0)

    dq_scaled = turn_back((dq_acc[...] * SCALE).T, cosine, sine)
    product = dq_scaled * q_normed
    own_q[...] += jnp.sum(product.reshape(QROWS // 8, 8, DH), 0)
    grad_normed = dq_scaled * gain
    inner = jnp.mean(grad_normed * q_normed, -1, keepdims=True)
    dq = unstacked((q_inverse * (grad_normed - q_normed * inner)).astype(jnp.bfloat16))

    @pl.when(own)
    def _():
        att_own[...] = att
        dq_own[...] = dq

    @pl.when(jnp.logical_not(own))
    def _():
        att_far[...] = att
        dq_far[...] = dq

    def write(column):
        for a in range(SHARDS):
            for b in range(2):
                src = pl.ds(pl.multiple_of(blk[2 * a + b] * RUN, RUN), RUN)
                rows = slice(b * RUN, (b + 1) * RUN)
                outs[a][rows, column * DH : (column + 1) * DH] = dk[src, :].astype(jnp.bfloat16)
                outs[a][rows, (2 + column) * DH : (3 + column) * DH] = dv[src, :].astype(jnp.bfloat16)

    @pl.when(run == 3)
    def _():
        k_gain = gains[0, 1:2, :]
        for j in range(NKB):
            rows = slice(j * KB, (j + 1) * KB)
            c, s = cos_sin(tab[rows, :])
            scaled = dk[rows, :] * SCALE
            dk[rows, :] = scaled
            normed = turn_back(ks[rows, :].astype(jnp.float32), c, s)
            own_k[...] += jnp.sum((turn_back(scaled, c, s) * normed).reshape(KB // 8, 8, DH), 0)

        @pl.when(head == 0)
        def _():
            write(0)

        @pl.when(head == 1)
        def _():
            write(1)
            sums = jnp.concatenate(
                [
                    jnp.sum(own_q[...], 0, keepdims=True),
                    jnp.sum(own_k[...], 0, keepdims=True) / k_gain,
                ],
                0,
            )
            own_out[...] = sums
            for a in range(SHARDS):
                outs[a][TOK:, :] = jnp.zeros((PAD, 4 * DH), jnp.bfloat16)


def attention(blk, side, query, q_far, out_grad, g_far, tab, gains, shards):
    width = GROUP * DH
    near = pl.BlockSpec((1, RUN, width), lambda g, r, b, s: (0, jnp.minimum(r, 1), s[0] * 2 + g))
    far = pl.BlockSpec((RUN, width), lambda g, r, b, s: (jnp.maximum(r - 2, 0), g))
    own = pl.BlockSpec((RUN, width), lambda g, r, b, s: (jnp.minimum(r, 1), g))
    block = pl.BlockSpec((TOK + PAD, 4 * DH), lambda g, r, b, s: (0, 0))
    half = jax.ShapeDtypeStruct((TOK, HALF), jnp.bfloat16)
    shard = jax.ShapeDtypeStruct((TOK + PAD, 4 * DH), jnp.bfloat16)
    low, full = jnp.bfloat16, jnp.float32
    result = pl.pallas_call(
        attention_kernel,
        out_shape=(half, half, half, half) + (shard,) * SHARDS + (jax.ShapeDtypeStruct((2, DH), full),),
        grid_spec=pltpu.PrefetchScalarGridSpec(
            num_scalar_prefetch=2,
            grid=(2, 4),
            in_specs=[
                near,
                far,
                near,
                far,
                pl.BlockSpec((SEQ, DH), lambda g, r, b, s: (0, 0)),
                pl.BlockSpec((1, 2, DH), lambda g, r, b, s: (0, 0, 0)),
            ]
            + [block] * SHARDS,
            out_specs=(own, far, own, far) + (block,) * SHARDS + (pl.BlockSpec((2, DH), lambda g, r, b, s: (0, 0)),),
            scratch_shapes=[
                pltpu.VMEM((SEQ, DH), low),
                pltpu.VMEM((SEQ, DH), low),
                pltpu.VMEM((NKB, DH, KB), low),
                pltpu.VMEM((NKB, DH, KB), low),
                pltpu.VMEM((SEQ, QROWS), full),
                pltpu.VMEM((SEQ, QROWS), low),
                pltpu.VMEM((SEQ, DH), full),
                pltpu.VMEM((SEQ, DH), full),
                pltpu.VMEM((DH, QROWS), full),
                pltpu.VMEM((DH, QROWS), full),
                pltpu.VMEM((8, DH), full),
                pltpu.VMEM((8, DH), full),
            ],
        ),
        compiler_params=pltpu.CompilerParams(vmem_limit_bytes=48 * 1024 * 1024),
        name="attention",
    )(blk, side, query, q_far, out_grad, g_far, tab, gains, *shards)
    return result[:4], result[4 : 4 + SHARDS], result[4 + SHARDS]


def finish_kernel(pos, side, key, tab, gains, near, far, key_grad, value_grad):
    cosine, sine = cos_sin(tab[...])
    gain = gains[0, 1:2, :]
    upper = side[0] == 1
    a = near[...]
    b = far[...].astype(jnp.float32)
    first = jnp.where(upper, b, a)
    second = jnp.where(upper, a, b)
    both = (first, second)
    for head in range(HK):
        half, place = both[head // 2], head % 2
        lanes = slice(head * DH, (head + 1) * DH)
        x = key[0, :, lanes].astype(jnp.float32)
        inverse = lax.rsqrt(jnp.mean(x * x, -1, keepdims=True) + EPS)
        normed = x * inverse
        scaled = turn_back(half[:, place * DH : (place + 1) * DH], cosine, sine)
        grad_normed = scaled * gain
        inner = jnp.mean(grad_normed * normed, -1, keepdims=True)
        key_grad[0, :, lanes] = (inverse * (grad_normed - normed * inner)).astype(jnp.bfloat16)
        value_grad[0, :, lanes] = half[:, (2 + place) * DH : (3 + place) * DH].astype(jnp.bfloat16)


def finish(positions, side, key, tab, gains, near, far):
    out = jax.ShapeDtypeStruct((1, TOK, HK * DH), jnp.bfloat16)
    rows = pl.BlockSpec((1, RUN, HK * DH), lambda r, p, s: (0, r, 0))
    block = pl.BlockSpec((RUN, 4 * DH), lambda r, p, s: (r, 0))
    return pl.pallas_call(
        finish_kernel,
        out_shape=(out, out),
        grid_spec=pltpu.PrefetchScalarGridSpec(
            num_scalar_prefetch=2,
            grid=(2,),
            in_specs=[
                rows,
                pl.BlockSpec((RUN, DH), lambda r, p, s: (p[0, r * RUN] // RUN, 0)),
                pl.BlockSpec((1, 2, DH), lambda r, p, s: (0, 0, 0)),
                block,
                block,
            ],
            out_specs=(rows, rows),
        ),
        name="finish",
    )(positions, side, key, tab, gains, near, far)


def along_z(x, by, depth):
    pairs = [(s * depth + z, s * depth + (z + by) % depth) for s in range(2) for z in range(depth)]
    return lax.ppermute(x, "ctx", pairs)


def across(x, depth):
    return lax.ppermute(x, "ctx", [(i, (i + depth) % (2 * depth)) for i in range(2 * depth)])


def body(query, key, value, out_grad, positions, gains):
    count = lax.axis_size("ctx")
    depth = count // 2
    pipes = lax.axis_size("pipe")
    upper = lax.axis_index("ctx") // depth
    side = upper.astype(jnp.int32).reshape(1)
    tab = jnp.asarray(rope_table())
    mine, other = prep(positions, side, key, value, tab, gains)

    got = across(other, depth)
    start = (1 - upper) * HALF
    q_far = across(lax.dynamic_slice(query[0], (0, start), (TOK, HALF)), depth)
    g_far = across(lax.dynamic_slice(out_grad[0], (0, start), (TOK, HALF)), depth)

    def gather(block):
        ups, downs = [], []
        up = down = block
        for step in range(4):
            up = along_z(up, 1, depth)
            ups.append(up)
            if step < 3:
                down = along_z(down, -1, depth)
                downs.append(down)
        return ups, downs

    ups_a, downs_a = gather(mine)
    ups_b, downs_b = gather(got)
    pairs = [(mine, got)] + list(zip(ups_a, ups_b)) + list(zip(downs_a, downs_b))
    shards = [s for pair in pairs for s in pair]
    blk = jnp.stack([s[TOK, :2] for s in shards]).reshape(2 * SHARDS).astype(jnp.int32)

    halves, grads, own = attention(blk, side, query, q_far, out_grad, g_far, tab, gains, shards)
    att_own, att_far, dq_own, dq_far = halves
    att_got = across(att_far, depth)
    dq_got = across(dq_far, depth)

    high = own.astype(jnp.bfloat16)
    rest = (own - high.astype(jnp.float32)).astype(jnp.bfloat16)
    terms = jnp.concatenate([high, rest], 0)

    def scatter(column):
        part = [grads[2 * i + column] for i in range(8)]
        ups, downs = part[1:5], part[5:8]
        carry_terms = column == 1
        down, up = ups[3], downs[2]
        if carry_terms:
            down = lax.dynamic_update_slice(down, terms, (TOK, 0))
            up = lax.dynamic_update_slice(up, terms, (TOK, 0))
        heard = []
        total = part[0][:TOK].astype(jnp.float32)
        for step in range(4):
            down = along_z(down, -1, depth)
            heard.append(down[TOK : TOK + 4, :DH])
            if step < 3:
                down = (down.astype(jnp.float32) + ups[2 - step].astype(jnp.float32)).astype(jnp.bfloat16)
                up = along_z(up, 1, depth)
                heard.append(up[TOK : TOK + 4, :DH])
                if step < 2:
                    up = (up.astype(jnp.float32) + downs[1 - step].astype(jnp.float32)).astype(jnp.bfloat16)
        total = total + down[:TOK].astype(jnp.float32) + up[:TOK].astype(jnp.float32)
        return total, heard

    far_total, heard = scatter(1)
    near_total, _ = scatter(0)
    gain_sum = own
    for h in heard:
        gain_sum = gain_sum + h[:2].astype(jnp.float32) + h[2:].astype(jnp.float32)

    back = across(far_total.astype(jnp.bfloat16), depth)
    gain_sum = gain_sum + across(gain_sum, depth)
    mirrored = lax.ppermute(gain_sum, "pipe", [(i, pipes - 1 - i) for i in range(pipes)])
    gain_grad = gain_sum + mirrored

    key_grad, value_grad = finish(positions, side, key, tab, gains, near_total, back)

    def joined(near, far):
        lower = jnp.concatenate([near, far], 1)
        higher = jnp.concatenate([far, near], 1)
        return jnp.where(upper == 0, lower, higher)[None]

    return (
        joined(att_own, att_got),
        joined(dq_own, dq_got),
        key_grad,
        value_grad,
        gain_grad[None],
    )


def solution(mesh):
    seq = P("pipe", "ctx", None)
    in_specs = (seq, seq, seq, seq, P("pipe", "ctx"), P("pipe", None, None))
    out_specs = (seq, seq, seq, seq, P("pipe", None, None))
    return jax.shard_map(body, mesh=mesh, in_specs=in_specs, out_specs=out_specs, check_vma=False)
```

```python
import jax
import jax.numpy as jnp
import numpy as np
from jax import lax
from jax.experimental import pallas as pl
from jax.experimental.pallas import tpu as pltpu
from jax.sharding import PartitionSpec as P

HQ = 32
HK = 4
DH = 128
THETA = 1000000.0
EPS = 1e-06
NEG = -1e30

TOK = 128
RUN = 64
SEQ = 2048
PAD = 16
GROUP = 8
QROWS = RUN * GROUP
KB = 256
NKB = SEQ // KB
HALF = HQ * DH // 2
SCALE = DH**-0.5
SCALE2 = SCALE * 1.4426950408889634
SHARDS = 8
PACK = 2 * TOK + PAD
BODY = 4
STARTS = (4, 7)


def rope_table():
    freq = (THETA ** (-(np.arange(DH // 2, dtype=np.float64) * 2.0) / DH)).astype(np.float32)
    turn = np.arange(SEQ, dtype=np.float32)[:, None] * freq[None, :]
    turn = turn.astype(np.float64)
    return np.concatenate([np.cos(turn), np.sin(turn)], -1).astype(np.float32)


def dot(a, b, dims=((1,), (0,))):
    return lax.dot_general(a, b, (dims, ((), ())), preferred_element_type=jnp.float32)


NT = ((1,), (1,))


def cos_sin(tab):
    low = lax.broadcasted_iota(jnp.int32, tab.shape, 1) < DH // 2
    other = pltpu.roll(tab, DH // 2, 1)
    return jnp.where(low, tab, other), jnp.where(low, -other, tab)


def turn_by(x, cosine, sine):
    return x * cosine + pltpu.roll(x, DH // 2, 1) * sine


def turn_back(x, cosine, sine):
    return x * cosine - pltpu.roll(x, DH // 2, 1) * sine


def hbm(shape, dtype):
    return pltpu.HBM(shape, dtype)


def whole(shape):
    return pl.BlockSpec(shape, lambda *_: (0,) * len(shape))


def prep_kernel(pos, side, key, value, query, grad, tab, gains, mine, other, q_out, g_out):
    run = pl.program_id(0)
    cosine, sine = cos_sin(tab[...])
    gain = gains[0, 1:2, :]
    pieces = []
    for head in range(HK):
        x = key[0, :, head * DH : (head + 1) * DH].astype(jnp.float32)
        inverse = lax.rsqrt(jnp.mean(x * x, -1, keepdims=True) + EPS)
        pieces.append(turn_by(x * inverse * gain, cosine, sine).astype(jnp.bfloat16))
    v = value[0]
    halves = (
        jnp.concatenate(pieces[:2] + [v[:, : 2 * DH]], -1),
        jnp.concatenate(pieces[2:] + [v[:, 2 * DH :]], -1),
    )
    rows = pl.ds(pl.multiple_of(run * RUN, RUN), RUN)
    upper = side[0] == 1
    mine[rows, :] = jnp.where(upper, halves[1], halves[0])
    other[rows, :] = jnp.where(upper, halves[0], halves[1])
    q_out[...] = query[0]
    g_out[...] = grad[0]

    @pl.when(run == 0)
    def _():
        lane = lax.broadcasted_iota(jnp.int32, (PAD, 4 * DH), 1)
        a = (pos[0, 0] // RUN).astype(jnp.float32)
        b = (pos[0, RUN] // RUN).astype(jnp.float32)
        mine[TOK:, :] = jnp.where(lane == 0, a, jnp.where(lane == 1, b, 0.0)).astype(jnp.bfloat16)
        other[TOK:, :] = jnp.where(lane == 2, a, jnp.where(lane == 3, b, 0.0)).astype(jnp.bfloat16)


def prep(positions, side, key, value, query, grad, tab, gains):
    rows = pl.BlockSpec((1, RUN, HK * DH), lambda r, p, s: (0, r, 0))
    other = pl.BlockSpec((1, RUN, HALF), lambda r, p, s: (0, r, 1 - s[0]))
    half = pl.BlockSpec((RUN, HALF), lambda r, p, s: (r, 0))
    shape = (TOK + PAD, 4 * DH)
    return pl.pallas_call(
        prep_kernel,
        out_shape=(
            hbm(shape, jnp.bfloat16),
            hbm(shape, jnp.bfloat16),
            hbm((TOK, HALF), jnp.bfloat16),
            hbm((TOK, HALF), jnp.bfloat16),
        ),
        grid_spec=pltpu.PrefetchScalarGridSpec(
            num_scalar_prefetch=2,
            grid=(2,),
            in_specs=[
                rows,
                rows,
                other,
                other,
                pl.BlockSpec((RUN, DH), lambda r, p, s: (p[0, r * RUN] // RUN, 0)),
                whole((1, 2, DH)),
            ],
            out_specs=(whole(shape), whole(shape), half, half),
        ),
        name="prep",
    )(positions, side, key, value, query, grad, tab, gains)


def stacked(x):
    return jnp.concatenate([x[:, h * DH : (h + 1) * DH] for h in range(GROUP)], 0)


def unstacked(x):
    return jnp.concatenate([x[h * RUN : (h + 1) * RUN] for h in range(GROUP)], 1)


def attention_kernel(blk, *refs):
    q_own, q_far, g_own, g_far, tab, gains = refs[:6]
    shards = refs[6 : 6 + SHARDS]
    att_own, att_far, dq_own, dq_far = refs[6 + SHARDS : 10 + SHARDS]
    outs = refs[10 + SHARDS : 10 + 2 * SHARDS]
    (ks, vs, kt, vt, scores, probs, dk, dv, o_acc, dq_acc, top8, sum8, own_q) = refs[10 + 2 * SHARDS :]
    run = pl.program_id(0)
    own = run < 2
    heads = (0, 1)

    def sorted_rows(a, b):
        return pl.ds(pl.multiple_of(blk[4 * a + b] * RUN, RUN), RUN)

    @pl.when(run == 0)
    def _():
        for a in range(SHARDS):
            for b in range(4):
                to = sorted_rows(a, b)
                for h in heads:
                    rows = slice(b * RUN, (b + 1) * RUN)
                    ks[h, to, :] = shards[a][rows, h * DH : (h + 1) * DH]
                    vs[h, to, :] = shards[a][rows, (2 + h) * DH : (3 + h) * DH]
        for h in heads:
            for j in range(NKB):
                kt[h, j] = ks[h, j * KB : (j + 1) * KB, :].T
                vt[h, j] = vs[h, j * KB : (j + 1) * KB, :].T
        dk[...] = jnp.zeros_like(dk)
        dv[...] = jnp.zeros_like(dv)
        own_q[...] = jnp.zeros_like(own_q)

    number = blk[run]
    cosine, sine = cos_sin(tab[pl.ds(pl.multiple_of(number * RUN, RUN), RUN), :])
    cosine = jnp.concatenate([cosine] * GROUP, 0)
    sine = jnp.concatenate([sine] * GROUP, 0)
    q_gain, k_gain = gains[0, 0:1, :], gains[0, 1:2, :]

    def half(near, far, h):
        lanes = slice(h * GROUP * DH, (h + 1) * GROUP * DH)
        return stacked(jnp.where(own, near[0, :, lanes], far[:, lanes]))

    q_rot, q_t, g_t = [], [], []
    for h in heads:
        x = half(q_own, q_far, h).astype(jnp.float32)
        q_inverse = lax.rsqrt(jnp.mean(x * x, -1, keepdims=True) + EPS)
        normed = x * q_inverse
        rot = turn_by(normed * q_gain, cosine, sine).astype(jnp.bfloat16)
        q_rot.append(rot)
        q_t.append(rot.T)
        g_t.append(half(g_own, g_far, h).T)

    last = number // (KB // RUN)
    lane = lax.broadcasted_iota(jnp.int32, (KB, QROWS), 1)
    row = lax.broadcasted_iota(jnp.int32, (KB, QROWS), 0)
    seen = row + last * KB <= number * RUN + (lane & (RUN - 1))

    def at(j):
        return pl.ds(pl.multiple_of(j * KB, KB), KB)

    def over(count, step):
        def several(i, carry):
            for n in range(BODY):
                step(BODY * i + n)
            return carry

        lax.fori_loop(0, count // BODY, several, 0)
        width = BODY // 2
        while width:

            @pl.when((count & width) != 0)
            def _(width=width):
                for n in range(width):
                    step((count // (2 * width)) * (2 * width) + n)

            width //= 2

    def fold(x, op):
        return op(x.reshape(KB // 8, 8, QROWS), 0)

    for h in heads:
        s = jnp.where(seen, dot(ks[h, at(last), :], q_t[h]) * SCALE2, NEG)
        scores[h, at(last), :] = s
        top8[h] = fold(s, jnp.max)

    def pass_a(j):
        for h in heads:
            s = dot(ks[h, at(j), :], q_t[h]) * SCALE2
            scores[h, at(j), :] = s
            top8[h] = jnp.maximum(top8[h], fold(s, jnp.max))

    over(last, pass_a)
    top = [jnp.max(top8[h], 0, keepdims=True) for h in heads]

    o_acc[...] = jnp.zeros_like(o_acc)
    sum8[...] = jnp.zeros_like(sum8)

    def pass_b(j):
        for h in heads:
            expo = jnp.exp2(scores[h, at(j), :] - top[h])
            low = expo.astype(jnp.bfloat16)
            probs[h, at(j), :] = low
            o_acc[h] += dot(vt[h, j], low)
            sum8[h] += fold(expo, jnp.sum)

    over(last + 1, pass_b)

    att, g_low, g_nat, delta = [], [], [], []
    for h in heads:
        inverse = 1.0 / jnp.sum(sum8[h], 0, keepdims=True)
        att_t = (o_acc[h] * inverse).astype(jnp.bfloat16)
        att.append(unstacked(att_t.T))
        low = (g_t[h].astype(jnp.float32) * inverse).astype(jnp.bfloat16)
        g_low.append(low)
        g_nat.append(low.T)
        delta.append(jnp.sum(low.astype(jnp.float32) * att_t.astype(jnp.float32), 0, keepdims=True))
    att = jnp.concatenate(att, 1)

    @pl.when(own)
    def _():
        att_own[...] = att

    @pl.when(jnp.logical_not(own))
    def _():
        att_far[...] = att

    dq_acc[...] = jnp.zeros_like(dq_acc)

    def pass_c(j):
        for h in heads:
            p = probs[h, at(j), :]
            d_prob = dot(vs[h, at(j), :], g_low[h])
            d_score = (p.astype(jnp.float32) * (d_prob - delta[h])).astype(jnp.bfloat16)
            dv[h, at(j), :] += dot(p, g_nat[h])
            dk[h, at(j), :] += dot(d_score, q_rot[h])
            dq_acc[h] += dot(kt[h, j], d_score)

    over(last + 1, pass_c)

    dq = []
    for h in heads:
        x = half(q_own, q_far, h).astype(jnp.float32)
        q_inverse = lax.rsqrt(jnp.mean(x * x, -1, keepdims=True) + EPS)
        normed = x * q_inverse
        dq_scaled = turn_back((dq_acc[h] * SCALE).T, cosine, sine)
        own_q[...] += jnp.sum((dq_scaled * normed).reshape(QROWS // 8, 8, DH), 0)
        grad_normed = dq_scaled * q_gain
        inner = jnp.mean(grad_normed * normed, -1, keepdims=True)
        dq.append(unstacked((q_inverse * (grad_normed - normed * inner)).astype(jnp.bfloat16)))
    dq = jnp.concatenate(dq, 1)

    @pl.when(own)
    def _():
        dq_own[...] = dq

    @pl.when(jnp.logical_not(own))
    def _():
        dq_far[...] = dq

    @pl.when(run == 3)
    def _():
        sums = jnp.zeros((8, DH), jnp.float32)
        for j in range(NKB):
            rows = slice(j * KB, (j + 1) * KB)
            c, s = cos_sin(tab[rows, :])
            for h in heads:
                scaled = dk[h, rows, :] * SCALE
                dk[h, rows, :] = scaled
                normed = turn_back(ks[h, rows, :].astype(jnp.float32), c, s)
                sums += jnp.sum((turn_back(scaled, c, s) * normed).reshape(KB // 8, 8, DH), 0)
        q_term = jnp.sum(own_q[...], 0, keepdims=True)
        k_term = jnp.sum(sums, 0, keepdims=True) / k_gain
        pair = jnp.concatenate([q_term, k_term], 0)
        high = pair.astype(jnp.bfloat16)
        rest = (pair - high.astype(jnp.float32)).astype(jnp.bfloat16)
        zero = jnp.zeros((PAD, DH), jnp.float32)
        rest = jnp.concatenate([rest.astype(jnp.float32), zero[2:]], 0).astype(jnp.bfloat16)
        high = jnp.concatenate([high.astype(jnp.float32), zero[2:]], 0).astype(jnp.bfloat16)
        zero = zero.astype(jnp.bfloat16)
        terms = jnp.concatenate([high, rest, zero, zero], 1)
        for a in range(SHARDS):
            outs[a][2 * TOK :, :] = terms if a in STARTS else jnp.zeros_like(terms)
            for b in range(4):
                rows = slice(b * RUN, (b + 1) * RUN)
                for h in heads:
                    outs[a][rows, h * DH : (h + 1) * DH] = dk[h, sorted_rows(a, b), :].astype(jnp.bfloat16)
                    outs[a][rows, (2 + h) * DH : (3 + h) * DH] = dv[h, sorted_rows(a, b), :].astype(jnp.bfloat16)


def attention(blk, side, query, q_far, out_grad, g_far, tab, gains, shards):
    near = pl.BlockSpec((1, RUN, HALF), lambda r, b, s: (0, jnp.minimum(r, 1), s[0]))
    far = pl.BlockSpec((RUN, HALF), lambda r, b, s: (jnp.maximum(r - 2, 0), 0))
    own = pl.BlockSpec((RUN, HALF), lambda r, b, s: (jnp.minimum(r, 1), 0))
    half = hbm((TOK, HALF), jnp.bfloat16)
    low, full = jnp.bfloat16, jnp.float32
    shape = (PACK, 4 * DH)

    def kernel(blk, side, *refs):
        attention_kernel(blk, *refs)

    result = pl.pallas_call(
        kernel,
        out_shape=(half, half, half, half) + (hbm(shape, low),) * SHARDS,
        grid_spec=pltpu.PrefetchScalarGridSpec(
            num_scalar_prefetch=2,
            grid=(4,),
            in_specs=[near, far, near, far, whole((SEQ, DH)), whole((1, 2, DH))] + [whole(shape)] * SHARDS,
            out_specs=(own, far, own, far) + (whole(shape),) * SHARDS,
            scratch_shapes=[
                pltpu.VMEM((2, SEQ, DH), low),
                pltpu.VMEM((2, SEQ, DH), low),
                pltpu.VMEM((2, NKB, DH, KB), low),
                pltpu.VMEM((2, NKB, DH, KB), low),
                pltpu.VMEM((2, SEQ, QROWS), full),
                pltpu.VMEM((2, SEQ, QROWS), low),
                pltpu.VMEM((2, SEQ, DH), full),
                pltpu.VMEM((2, SEQ, DH), full),
                pltpu.VMEM((2, DH, QROWS), full),
                pltpu.VMEM((2, DH, QROWS), full),
                pltpu.VMEM((2, 8, QROWS), full),
                pltpu.VMEM((2, 8, QROWS), full),
                pltpu.VMEM((8, DH), full),
            ],
        ),
        compiler_params=pltpu.CompilerParams(vmem_limit_bytes=50 * 1024 * 1024),
        cost_estimate=pl.CostEstimate(flops=20_000_000_000, bytes_accessed=8_000_000, transcendentals=8_000_000),
        name="attention",
    )(blk, side, query, q_far, out_grad, g_far, tab, gains, *shards)
    return result[:4], result[4:]


def finish_kernel(pos, side, key, tab, gains, near, down, up, far, key_grad, value_grad):
    cosine, sine = cos_sin(tab[...])
    gain = gains[0, 1:2, :]
    upper = side[0] == 1
    a = near[...].astype(jnp.float32) + down[...].astype(jnp.float32) + up[...].astype(jnp.float32)
    b = far[...].astype(jnp.float32)
    both = (jnp.where(upper, b, a), jnp.where(upper, a, b))
    for head in range(HK):
        total, spot = both[head // 2], head % 2
        lanes = slice(head * DH, (head + 1) * DH)
        x = key[0, :, lanes].astype(jnp.float32)
        inverse = lax.rsqrt(jnp.mean(x * x, -1, keepdims=True) + EPS)
        normed = x * inverse
        scaled = turn_back(total[:, spot * DH : (spot + 1) * DH], cosine, sine)
        grad_normed = scaled * gain
        inner = jnp.mean(grad_normed * normed, -1, keepdims=True)
        key_grad[0, :, lanes] = (inverse * (grad_normed - normed * inner)).astype(jnp.bfloat16)
        value_grad[0, :, lanes] = total[:, (2 + spot) * DH : (3 + spot) * DH].astype(jnp.bfloat16)


def finish(positions, side, key, tab, gains, near, far):
    rows = pl.BlockSpec((1, RUN, HK * DH), lambda r, p, s: (0, r, 0))
    block = pl.BlockSpec((RUN, 4 * DH), lambda r, p, s: (r, 0))
    out = hbm((1, TOK, HK * DH), jnp.bfloat16)
    return pl.pallas_call(
        finish_kernel,
        out_shape=(out, out),
        grid_spec=pltpu.PrefetchScalarGridSpec(
            num_scalar_prefetch=2,
            grid=(2,),
            in_specs=[
                rows,
                pl.BlockSpec((RUN, DH), lambda r, p, s: (p[0, r * RUN] // RUN, 0)),
                whole((1, 2, DH)),
            ]
            + [block] * 4,
            out_specs=(rows, rows),
        ),
        name="finish",
    )(positions, side, key, tab, gains, *near, far)


def body(query, key, value, out_grad, positions, gains):
    count = lax.axis_size("ctx")
    depth = count // 2
    pipes = lax.axis_size("pipe")
    index = lax.axis_index("ctx").astype(jnp.int32)
    side = (index // depth).reshape(1)
    tab = jnp.asarray(rope_table())

    def across(x):
        return lax.ppermute(x, "ctx", [(i, (i + depth) % count) for i in range(count)])

    def along(x, by):
        return lax.ppermute(
            x, "ctx", [(s * depth + z, s * depth + (z + by) % depth) for s in range(2) for z in range(depth)]
        )

    mine, other, q_send, g_send = prep(positions, side, key, value, query, out_grad, tab, gains)
    got = across(other)
    q_far, g_far = across(q_send), across(g_send)
    both = jnp.concatenate([mine[:TOK], got[:TOK], mine[TOK:] + got[TOK:]], 0)
    up = down = both
    ups, downs = [], []
    for step in range(4):
        up = along(up, 1)
        if step in (1, 2):
            up = lax.dynamic_update_slice(up, (q_far, g_far)[step - 1][:8, :DH], (2 * TOK + 8, 0))
        ups.append(up)
        if step < 3:
            down = along(down, -1)
            downs.append(down)
    shards = [both] + ups + downs
    blk = jnp.stack([s[2 * TOK, :4] for s in shards]).reshape(4 * SHARDS).astype(jnp.int32)

    (att_own, att_far, dq_own, dq_far), grads = attention(
        blk, side, query, q_far, out_grad, g_far, tab, gains, shards
    )

    def added(a, b):
        return (a.astype(jnp.float32) + b.astype(jnp.float32)).astype(jnp.bfloat16)

    ups, downs = grads[1:5], grads[5:8]
    down, up = ups[3], downs[2]
    heard = [down]
    for step in range(4):
        down = along(down, -1)
        heard.append(down)
        if step < 3:
            down = added(down, ups[2 - step])
            up = along(up, 1)
            heard.append(up)
            if step < 2:
                up = added(up, downs[1 - step])
    att_got, dq_got = across(att_far), across(dq_far)

    def summed(rows):
        a, b, c = (x[rows].astype(jnp.float32) for x in (grads[0], down, up))
        return (a + b + c).astype(jnp.bfloat16)

    def two_parts(x):
        high = x.astype(jnp.bfloat16)
        return jnp.concatenate([high, (x - high.astype(jnp.float32)).astype(jnp.bfloat16)], 1)

    def one_part(x):
        x = x.astype(jnp.float32)
        return x[:, :DH] + x[:, DH:]

    column_sum = one_part(sum(h[2 * TOK : 2 * TOK + 2, : 2 * DH].astype(jnp.float32) for h in heard))
    leaving = lax.dynamic_update_slice(summed(slice(TOK, PACK)), two_parts(column_sum), (TOK, 0))
    back = across(leaving)
    gain_sum = column_sum + one_part(back[TOK : TOK + 2, : 2 * DH])
    mirrored = lax.ppermute(gain_sum, "pipe", [(i, pipes - 1 - i) for i in range(pipes)])
    gain_grad = gain_sum + mirrored

    key_grad, value_grad = finish(positions, side, key, tab, gains, (grads[0], down, up), back)

    def joined(near, far):
        upper = side[0] == 1
        return jnp.concatenate([jnp.where(upper, far, near), jnp.where(upper, near, far)], 1)[None]

    return joined(att_own, att_got), joined(dq_own, dq_got), key_grad, value_grad, gain_grad[None]


def solution(mesh):
    seq = P("pipe", "ctx", None)
    in_specs = (seq, seq, seq, seq, P("pipe", "ctx"), P("pipe", None, None))
    out_specs = (seq, seq, seq, seq, P("pipe", None, None))
    return jax.shard_map(body, mesh=mesh, in_specs=in_specs, out_specs=out_specs, check_vma=False)
```

```python
import jax
import jax.numpy as jnp
import numpy as np
from jax import lax
from jax.experimental import pallas as pl
from jax.experimental.pallas import tpu as pltpu
from jax.sharding import PartitionSpec as P

HQ = 32
HK = 4
DH = 128
THETA = 1000000.0
EPS = 1e-06
NEG = -1e30

TOK = 128
RUN = 64
SEQ = 2048
PAD = 16
GROUP = 8
QROWS = RUN * GROUP
KB = 256
NKB = SEQ // KB
HALF = HQ * DH // 2
SCALE = DH**-0.5
SCALE2 = SCALE * 1.4426950408889634
SHARDS = 8
PACK = 2 * TOK + PAD
BODY = 4
STARTS = (4, 7)


def rope_table():
    freq = (THETA ** (-(np.arange(DH // 2, dtype=np.float64) * 2.0) / DH)).astype(np.float32)
    turn = np.arange(SEQ, dtype=np.float32)[:, None] * freq[None, :]
    turn = turn.astype(np.float64)
    return np.concatenate([np.cos(turn), np.sin(turn)], -1).astype(np.float32)


def dot(a, b, dims=((1,), (0,))):
    return lax.dot_general(a, b, (dims, ((), ())), preferred_element_type=jnp.float32)


NT = ((1,), (1,))


def cos_sin(tab):
    low = lax.broadcasted_iota(jnp.int32, tab.shape, 1) < DH // 2
    other = pltpu.roll(tab, DH // 2, 1)
    return jnp.where(low, tab, other), jnp.where(low, -other, tab)


def turn_by(x, cosine, sine):
    return x * cosine + pltpu.roll(x, DH // 2, 1) * sine


def turn_back(x, cosine, sine):
    return x * cosine - pltpu.roll(x, DH // 2, 1) * sine


def hbm(shape, dtype):
    return pltpu.HBM(shape, dtype)


def whole(shape):
    return pl.BlockSpec(shape, lambda *_: (0,) * len(shape))


def prep_kernel(pos, side, key, value, query, grad, tab, gains, mine, other, q_out, g_out):
    run = pl.program_id(0)
    cosine, sine = cos_sin(tab[...])
    gain = gains[0, 1:2, :]
    pieces = []
    for head in range(HK):
        x = key[0, :, head * DH : (head + 1) * DH].astype(jnp.float32)
        inverse = lax.rsqrt(jnp.mean(x * x, -1, keepdims=True) + EPS)
        pieces.append(turn_by(x * inverse * gain, cosine, sine).astype(jnp.bfloat16))
    v = value[0]
    halves = (
        jnp.concatenate(pieces[:2] + [v[:, : 2 * DH]], -1),
        jnp.concatenate(pieces[2:] + [v[:, 2 * DH :]], -1),
    )
    rows = pl.ds(pl.multiple_of(run * RUN, RUN), RUN)
    upper = side[0] == 1
    mine[rows, :] = jnp.where(upper, halves[1], halves[0])
    other[rows, :] = jnp.where(upper, halves[0], halves[1])
    q_out[...] = query[0]
    g_out[...] = grad[0]

    @pl.when(run == 0)
    def _():
        lane = lax.broadcasted_iota(jnp.int32, (PAD, 4 * DH), 1)
        a = (pos[0, 0] // RUN).astype(jnp.float32)
        b = (pos[0, RUN] // RUN).astype(jnp.float32)
        mine[TOK:, :] = jnp.where(lane == 0, a, jnp.where(lane == 1, b, 0.0)).astype(jnp.bfloat16)
        other[TOK:, :] = jnp.where(lane == 2, a, jnp.where(lane == 3, b, 0.0)).astype(jnp.bfloat16)


def prep(positions, side, key, value, query, grad, tab, gains):
    rows = pl.BlockSpec((1, RUN, HK * DH), lambda r, p, s: (0, r, 0))
    other = pl.BlockSpec((1, RUN, HALF), lambda r, p, s: (0, r, 1 - s[0]))
    half = pl.BlockSpec((RUN, HALF), lambda r, p, s: (r, 0))
    shape = (TOK + PAD, 4 * DH)
    return pl.pallas_call(
        prep_kernel,
        out_shape=(
            hbm(shape, jnp.bfloat16),
            hbm(shape, jnp.bfloat16),
            hbm((TOK, HALF), jnp.bfloat16),
            hbm((TOK, HALF), jnp.bfloat16),
        ),
        grid_spec=pltpu.PrefetchScalarGridSpec(
            num_scalar_prefetch=2,
            grid=(2,),
            in_specs=[
                rows,
                rows,
                other,
                other,
                pl.BlockSpec((RUN, DH), lambda r, p, s: (p[0, r * RUN] // RUN, 0)),
                whole((1, 2, DH)),
            ],
            out_specs=(whole(shape), whole(shape), half, half),
        ),
        name="prep",
    )(positions, side, key, value, query, grad, tab, gains)


def stacked(x):
    return jnp.concatenate([x[:, h * DH : (h + 1) * DH] for h in range(GROUP)], 0)


def unstacked(x):
    return jnp.concatenate([x[h * RUN : (h + 1) * RUN] for h in range(GROUP)], 1)


def attention_kernel(blk, *refs):
    q_own, q_far, g_own, g_far, tab, gains = refs[:6]
    shards = refs[6 : 6 + SHARDS]
    att_own, att_far, dq_own, dq_far = refs[6 + SHARDS : 10 + SHARDS]
    outs = refs[10 + SHARDS : 10 + 2 * SHARDS]
    (ks, vs, kt, vt, scores, probs, dk, dv, o_acc, dq_acc, top8, sum8, own_q) = refs[10 + 2 * SHARDS :]
    run = pl.program_id(0)
    own = run < 2
    heads = (0, 1)

    def sorted_rows(a, b):
        return pl.ds(pl.multiple_of(blk[4 * a + b] * RUN, RUN), RUN)

    @pl.when(run == 0)
    def _():
        for a in range(SHARDS):
            for b in range(4):
                to = sorted_rows(a, b)
                for h in heads:
                    rows = slice(b * RUN, (b + 1) * RUN)
                    ks[h, to, :] = shards[a][rows, h * DH : (h + 1) * DH]
                    vs[h, to, :] = shards[a][rows, (2 + h) * DH : (3 + h) * DH]
        for h in heads:
            for j in range(NKB):
                kt[h, j] = ks[h, j * KB : (j + 1) * KB, :].T
                vt[h, j] = vs[h, j * KB : (j + 1) * KB, :].T
        dk[...] = jnp.zeros_like(dk)
        dv[...] = jnp.zeros_like(dv)
        own_q[...] = jnp.zeros_like(own_q)

    number = blk[run]
    cosine, sine = cos_sin(tab[pl.ds(pl.multiple_of(number * RUN, RUN), RUN), :])
    cosine = jnp.concatenate([cosine] * GROUP, 0)
    sine = jnp.concatenate([sine] * GROUP, 0)
    q_gain, k_gain = gains[0, 0:1, :], gains[0, 1:2, :]

    def half(near, far, h):
        lanes = slice(h * GROUP * DH, (h + 1) * GROUP * DH)
        return stacked(jnp.where(own, near[0, :, lanes], far[:, lanes]))

    q_rot, q_t, g_t = [], [], []
    for h in heads:
        x = half(q_own, q_far, h).astype(jnp.float32)
        q_inverse = lax.rsqrt(jnp.mean(x * x, -1, keepdims=True) + EPS)
        normed = x * q_inverse
        rot = turn_by(normed * q_gain, cosine, sine).astype(jnp.bfloat16)
        q_rot.append(rot)
        q_t.append(rot.T)
        g_t.append(half(g_own, g_far, h).T)

    last = number // (KB // RUN)
    lane = lax.broadcasted_iota(jnp.int32, (KB, QROWS), 1)
    row = lax.broadcasted_iota(jnp.int32, (KB, QROWS), 0)
    seen = row + last * KB <= number * RUN + (lane & (RUN - 1))

    def at(j):
        return pl.ds(pl.multiple_of(j * KB, KB), KB)

    def over(count, step):
        def several(i, carry):
            for n in range(BODY):
                step(BODY * i + n)
            return carry

        lax.fori_loop(0, count // BODY, several, 0)
        width = BODY // 2
        while width:

            @pl.when((count & width) != 0)
            def _(width=width):
                for n in range(width):
                    step((count // (2 * width)) * (2 * width) + n)

            width //= 2

    def fold(x, op):
        return op(x.reshape(KB // 8, 8, QROWS), 0)

    for h in heads:
        s = jnp.where(seen, dot(ks[h, at(last), :], q_t[h]) * SCALE2, NEG)
        scores[h, at(last), :] = s
        top8[h] = fold(s, jnp.max)

    def pass_a(j):
        for h in heads:
            s = dot(ks[h, at(j), :], q_t[h]) * SCALE2
            scores[h, at(j), :] = s
            top8[h] = jnp.maximum(top8[h], fold(s, jnp.max))

    over(last, pass_a)
    top = [jnp.max(top8[h], 0, keepdims=True) for h in heads]

    o_acc[...] = jnp.zeros_like(o_acc)
    sum8[...] = jnp.zeros_like(sum8)

    def pass_b(j):
        for h in heads:
            expo = jnp.exp2(scores[h, at(j), :] - top[h])
            low = expo.astype(jnp.bfloat16)
            probs[h, at(j), :] = low
            o_acc[h] += dot(vt[h, j], low)
            sum8[h] += fold(expo, jnp.sum)

    over(last + 1, pass_b)

    att, g_low, g_nat, delta = [], [], [], []
    for h in heads:
        inverse = 1.0 / jnp.sum(sum8[h], 0, keepdims=True)
        att_t = (o_acc[h] * inverse).astype(jnp.bfloat16)
        att.append(unstacked(att_t.T))
        low = (g_t[h].astype(jnp.float32) * inverse).astype(jnp.bfloat16)
        g_low.append(low)
        g_nat.append(low.T)
        delta.append(jnp.sum(low.astype(jnp.float32) * att_t.astype(jnp.float32), 0, keepdims=True))
    att = jnp.concatenate(att, 1)

    @pl.when(own)
    def _():
        att_own[...] = att

    @pl.when(jnp.logical_not(own))
    def _():
        att_far[...] = att

    dq_acc[...] = jnp.zeros_like(dq_acc)

    def pass_c(j):
        for h in heads:
            p = probs[h, at(j), :]
            d_prob = dot(vs[h, at(j), :], g_low[h])
            d_score = (p.astype(jnp.float32) * (d_prob - delta[h])).astype(jnp.bfloat16)
            dv[h, at(j), :] += dot(p, g_nat[h])
            dk[h, at(j), :] += dot(d_score, q_rot[h])
            dq_acc[h] += dot(kt[h, j], d_score)

    over(last + 1, pass_c)

    dq = []
    for h in heads:
        x = half(q_own, q_far, h).astype(jnp.float32)
        q_inverse = lax.rsqrt(jnp.mean(x * x, -1, keepdims=True) + EPS)
        normed = x * q_inverse
        dq_scaled = turn_back((dq_acc[h] * SCALE).T, cosine, sine)
        own_q[...] += jnp.sum((dq_scaled * normed).reshape(QROWS // 8, 8, DH), 0)
        grad_normed = dq_scaled * q_gain
        inner = jnp.mean(grad_normed * normed, -1, keepdims=True)
        dq.append(unstacked((q_inverse * (grad_normed - normed * inner)).astype(jnp.bfloat16)))
    dq = jnp.concatenate(dq, 1)

    @pl.when(own)
    def _():
        dq_own[...] = dq

    @pl.when(jnp.logical_not(own))
    def _():
        dq_far[...] = dq

    @pl.when(run == 3)
    def _():
        sums = jnp.zeros((8, DH), jnp.float32)
        for j in range(NKB):
            rows = slice(j * KB, (j + 1) * KB)
            c, s = cos_sin(tab[rows, :])
            for h in heads:
                scaled = dk[h, rows, :] * SCALE
                dk[h, rows, :] = scaled
                normed = turn_back(ks[h, rows, :].astype(jnp.float32), c, s)
                sums += jnp.sum((turn_back(scaled, c, s) * normed).reshape(KB // 8, 8, DH), 0)
        q_term = jnp.sum(own_q[...], 0, keepdims=True)
        k_term = jnp.sum(sums, 0, keepdims=True) / k_gain
        pair = jnp.concatenate([q_term, k_term], 0)
        high = pair.astype(jnp.bfloat16)
        rest = (pair - high.astype(jnp.float32)).astype(jnp.bfloat16)
        zero = jnp.zeros((PAD, DH), jnp.float32)
        rest = jnp.concatenate([rest.astype(jnp.float32), zero[2:]], 0).astype(jnp.bfloat16)
        high = jnp.concatenate([high.astype(jnp.float32), zero[2:]], 0).astype(jnp.bfloat16)
        zero = zero.astype(jnp.bfloat16)
        terms = jnp.concatenate([high, rest, zero, zero], 1)
        for a in range(SHARDS):
            outs[a][2 * TOK :, :] = terms if a in STARTS else jnp.zeros_like(terms)
            for b in range(4):
                rows = slice(b * RUN, (b + 1) * RUN)
                for h in heads:
                    outs[a][rows, h * DH : (h + 1) * DH] = dk[h, sorted_rows(a, b), :].astype(jnp.bfloat16)
                    outs[a][rows, (2 + h) * DH : (3 + h) * DH] = dv[h, sorted_rows(a, b), :].astype(jnp.bfloat16)


def attention(blk, side, query, q_far, out_grad, g_far, tab, gains, shards):
    near = pl.BlockSpec((1, RUN, HALF), lambda r, b, s: (0, jnp.minimum(r, 1), s[0]))
    far = pl.BlockSpec((RUN, HALF), lambda r, b, s: (jnp.maximum(r - 2, 0), 0))
    own = pl.BlockSpec((RUN, HALF), lambda r, b, s: (jnp.minimum(r, 1), 0))
    half = hbm((TOK, HALF), jnp.bfloat16)
    low, full = jnp.bfloat16, jnp.float32
    shape = (PACK, 4 * DH)

    def kernel(blk, side, *refs):
        attention_kernel(blk, *refs)

    result = pl.pallas_call(
        kernel,
        out_shape=(half, half, half, half) + (hbm(shape, low),) * SHARDS,
        grid_spec=pltpu.PrefetchScalarGridSpec(
            num_scalar_prefetch=2,
            grid=(4,),
            in_specs=[near, far, near, far, whole((SEQ, DH)), whole((1, 2, DH))] + [whole(shape)] * SHARDS,
            out_specs=(own, far, own, far) + (whole(shape),) * SHARDS,
            scratch_shapes=[
                pltpu.VMEM((2, SEQ, DH), low),
                pltpu.VMEM((2, SEQ, DH), low),
                pltpu.VMEM((2, NKB, DH, KB), low),
                pltpu.VMEM((2, NKB, DH, KB), low),
                pltpu.VMEM((2, SEQ, QROWS), full),
                pltpu.VMEM((2, SEQ, QROWS), low),
                pltpu.VMEM((2, SEQ, DH), full),
                pltpu.VMEM((2, SEQ, DH), full),
                pltpu.VMEM((2, DH, QROWS), full),
                pltpu.VMEM((2, DH, QROWS), full),
                pltpu.VMEM((2, 8, QROWS), full),
                pltpu.VMEM((2, 8, QROWS), full),
                pltpu.VMEM((8, DH), full),
            ],
        ),
        compiler_params=pltpu.CompilerParams(vmem_limit_bytes=50 * 1024 * 1024),
        cost_estimate=pl.CostEstimate(flops=20_000_000_000, bytes_accessed=8_000_000, transcendentals=8_000_000),
        name="attention",
    )(blk, side, query, q_far, out_grad, g_far, tab, gains, *shards)
    return result[:4], result[4:]


def finish_kernel(pos, side, key, tab, gains, near, down, up, far, key_grad, value_grad):
    cosine, sine = cos_sin(tab[...])
    gain = gains[0, 1:2, :]
    upper = side[0] == 1
    a = near[...].astype(jnp.float32) + down[...].astype(jnp.float32) + up[...].astype(jnp.float32)
    b = far[...].astype(jnp.float32)
    both = (jnp.where(upper, b, a), jnp.where(upper, a, b))
    for head in range(HK):
        total, spot = both[head // 2], head % 2
        lanes = slice(head * DH, (head + 1) * DH)
        x = key[0, :, lanes].astype(jnp.float32)
        inverse = lax.rsqrt(jnp.mean(x * x, -1, keepdims=True) + EPS)
        normed = x * inverse
        scaled = turn_back(total[:, spot * DH : (spot + 1) * DH], cosine, sine)
        grad_normed = scaled * gain
        inner = jnp.mean(grad_normed * normed, -1, keepdims=True)
        key_grad[0, :, lanes] = (inverse * (grad_normed - normed * inner)).astype(jnp.bfloat16)
        value_grad[0, :, lanes] = total[:, (2 + spot) * DH : (3 + spot) * DH].astype(jnp.bfloat16)


def finish(positions, side, key, tab, gains, near, far):
    rows = pl.BlockSpec((1, RUN, HK * DH), lambda r, p, s: (0, r, 0))
    block = pl.BlockSpec((RUN, 4 * DH), lambda r, p, s: (r, 0))
    out = hbm((1, TOK, HK * DH), jnp.bfloat16)
    return pl.pallas_call(
        finish_kernel,
        out_shape=(out, out),
        grid_spec=pltpu.PrefetchScalarGridSpec(
            num_scalar_prefetch=2,
            grid=(2,),
            in_specs=[
                rows,
                pl.BlockSpec((RUN, DH), lambda r, p, s: (p[0, r * RUN] // RUN, 0)),
                whole((1, 2, DH)),
            ]
            + [block] * 4,
            out_specs=(rows, rows),
        ),
        name="finish",
    )(positions, side, key, tab, gains, *near, far)


def body(query, key, value, out_grad, positions, gains):
    count = lax.axis_size("ctx")
    depth = count // 2
    pipes = lax.axis_size("pipe")
    index = lax.axis_index("ctx").astype(jnp.int32)
    side = (index // depth).reshape(1)
    tab = jnp.asarray(rope_table())

    def across(x):
        return lax.ppermute(x, "ctx", [(i, (i + depth) % count) for i in range(count)])

    def along(x, by):
        return lax.ppermute(
            x, "ctx", [(s * depth + z, s * depth + (z + by) % depth) for s in range(2) for z in range(depth)]
        )

    mine, other, q_send, g_send = prep(positions, side, key, value, query, out_grad, tab, gains)
    got = across(other)
    q_far, g_far = across(q_send), across(g_send)
    both = jnp.concatenate([mine[:TOK], got[:TOK], mine[TOK:] + got[TOK:]], 0)
    up = down = both
    ups, downs = [], []
    for step in range(4):
        up = along(up, 1)
        if step in (1, 2):
            up = lax.dynamic_update_slice(up, (q_far, g_far)[step - 1][:8, :DH], (2 * TOK + 8, 0))
        ups.append(up)
        if step < 3:
            down = along(down, -1)
            downs.append(down)
    shards = [both] + ups + downs
    blk = jnp.stack([s[2 * TOK, :4] for s in shards]).reshape(4 * SHARDS).astype(jnp.int32)

    (att_own, att_far, dq_own, dq_far), grads = attention(
        blk, side, query, q_far, out_grad, g_far, tab, gains, shards
    )

    def added(a, b):
        return (a.astype(jnp.float32) + b.astype(jnp.float32)).astype(jnp.bfloat16)

    ups, downs = grads[1:5], grads[5:8]
    down, up = ups[3], downs[2]
    heard = [down]
    for step in range(4):
        down = along(down, -1)
        heard.append(down)
        if step < 3:
            down = added(down, ups[2 - step])
            up = along(up, 1)
            heard.append(up)
            if step < 2:
                up = added(up, downs[1 - step])
    att_got, dq_got = across(att_far), across(dq_far)

    def summed(rows):
        a, b, c = (x[rows].astype(jnp.float32) for x in (grads[0], down, up))
        return (a + b + c).astype(jnp.bfloat16)

    def two_parts(x):
        high = x.astype(jnp.bfloat16)
        return jnp.concatenate([high, (x - high.astype(jnp.float32)).astype(jnp.bfloat16)], 1)

    def one_part(x):
        x = x.astype(jnp.float32)
        return x[:, :DH] + x[:, DH:]

    column_sum = one_part(sum(h[2 * TOK : 2 * TOK + 2, : 2 * DH].astype(jnp.float32) for h in heard))
    leaving = lax.dynamic_update_slice(summed(slice(TOK, PACK)), two_parts(column_sum), (TOK, 0))
    back = across(leaving)
    tail = leaving[TOK:, : 2 * DH]

    def mirrored(by):
        pairs = [
            (p * count + i, (pipes - 1 - p) * count + (i + by) % count) for p in range(pipes) for i in range(count)
        ]
        return one_part(lax.ppermute(tail, ("pipe", "ctx"), pairs)[:2])

    gain_grad = column_sum + one_part(back[TOK : TOK + 2, : 2 * DH]) + (mirrored(0) + mirrored(depth))

    key_grad, value_grad = finish(positions, side, key, tab, gains, (grads[0], down, up), back)

    def joined(near, far):
        upper = side[0] == 1
        return jnp.concatenate([jnp.where(upper, far, near), jnp.where(upper, near, far)], 1)[None]

    return joined(att_own, att_got), joined(dq_own, dq_got), key_grad, value_grad, gain_grad[None]


def solution(mesh):
    seq = P("pipe", "ctx", None)
    in_specs = (seq, seq, seq, seq, P("pipe", "ctx"), P("pipe", None, None))
    out_specs = (seq, seq, seq, seq, P("pipe", None, None))
    return jax.shard_map(body, mesh=mesh, in_specs=in_specs, out_specs=out_specs, check_vma=False)
```
